32 devices in a mesh: group: 2 (over x), head: 16 (over z, y, core).
Axes of the slice: x: 2, y: 2, z: 4, core: 2. Of those that a mesh axis runs over, the one named last changes fastest.
Arguments:
- queries: bfloat16 [4096, 64, 192], P(('group', 'head')), parts along dimension 0, may hold values from -20 to 20
- latent: bfloat16 [4096, 512], P(('group', 'head')), parts along dimension 0, may hold values from -6 to 6
- rope_key: bfloat16 [4096, 64], P(('group', 'head')), parts along dimension 0, may hold values from -8 to 8
- key_up: bfloat16 [512, 64, 128], P(None, 'head'), may hold values from -0.25 to 0.25
- value_up: bfloat16 [512, 64, 128], P(None, 'head'), may hold values from -0.25 to 0.25
- first_key: int32 [4096], P('group'), parts along dimension 0, may hold values from 0 to 2047, as said below
- out_grad: bfloat16 [4096, 64, 128], P(('group', 'head')), parts along dimension 0, may hold values from -6 to 6
Outputs:
- query_grad: bfloat16 [4096, 64, 192], P(('group', 'head')), parts along dimension 0
- latent_grad: bfloat16 [4096, 512], P(('group', 'head')), parts along dimension 0
- rope_key_grad: bfloat16 [4096, 64], P(('group', 'head')), parts along dimension 0
- key_up_grad: float32 [1024, 64, 128], P('group', 'head'), parts along dimension 0
- value_up_grad: float32 [1024, 64, 128], P('group', 'head'), parts along dimension 0
The draws below stay inside these ranges and needn't reach their ends.
There are 2 independent parts, one for each index of `group`. The reference program is written for one: setup_inputs(seed, part) draws one part's arguments, and reference() takes and returns one part's arrays. A program takes and returns all parts, laid end to end along the dimension named above; an argument that names none is the same for every part. Nothing has to cross between parts.
Inputs may be any that keep to these rules, and one draw needn't show every extreme that they name: first_key never decreases as i grows, first_key[i] <= i, and i - first_key[i] < 512.
All inputs are finite; a program needn't handle non-finite values.
Results may differ from the reference program's by a relative error of at most 0.024.
Values may be sent and summed in bfloat16 or wider, within the bound.
A program may use at most 128 MiB of HBM per device.

```python
import math
import jax
import jax.numpy as jnp
from jax import lax

H = 64
LAT = 512
NOPE = 128
ROPE = 64
VD = 128
QK = 192
SEQ = 2048
QBLOCK = 512
SPAN = 512


def shared_draw(key):
    base = jax.random.fold_in(key, 71)
    keys_split = jax.random.split(base, 2)
    rotary = jnp.clip(jax.random.normal(keys_split[1], (SEQ, ROPE), jnp.float32), -6.0, 6.0)
    query_vals = jnp.clip(jax.random.normal(keys_split[0], (SEQ, H, QK), jnp.float32), -6.0, 6.0)
    return (query_vals, rotary)


def draw_queries(key, part):
    return shared_draw(key)[0].astype(jnp.bfloat16)


def draw_rope_key(key, part):
    return shared_draw(key)[1].astype(jnp.bfloat16)


def draw_first_key(key, part):
    stream = jax.random.fold_in(key, 5)
    cuts = jnp.sort(jax.random.randint(stream, (3,), SPAN, SEQ))
    position = jnp.arange(SEQ, dtype=jnp.int32)
    starts = jnp.max(jnp.where(cuts[None, :] <= position[:, None], cuts[None, :], 0), axis=1)
    return jnp.maximum(starts, position - SPAN + 1).astype(jnp.int32)


def block_levels(own_key, shape, pieces, smallest, high):
    level, own = 1.0, jax.random.fold_in(own_key, 6)
    for axis_at, shards_of in pieces:
        heights = jnp.exp(jax.random.uniform(jax.random.fold_in(own, axis_at), (shards_of,), jnp.float32, smallest / len(pieces), high / len(pieces)))
        level = level * jnp.repeat(heights, shape[axis_at] // shards_of).reshape([-1 if axis == axis_at else 1 for axis in range(len(shape))])
    return level


def gaussian(rng, extent, scale, reach, shards=(), held_as=jnp.bfloat16):
    values = scale * jax.random.normal(rng, extent, jnp.float32)
    if shards:
        values = values * block_levels(rng, extent, shards, -0.22, 0.18)
    return jnp.clip(values, -reach, reach).astype(held_as)


def setup_inputs(seed: int = 0, part: int = 0) -> dict:
    splits = jax.random.split(jax.random.key(seed), 8)
    own_keys = jax.random.split(jax.random.fold_in(splits[7], part), 8)
    return {
        "queries": draw_queries(jax.random.fold_in(jax.random.fold_in(splits[7], part), 71), part),
        "latent": gaussian(own_keys[1], (SEQ, LAT), 1.0, 6.0, ((0, 16),)),
        "rope_key": draw_rope_key(jax.random.fold_in(jax.random.fold_in(splits[7], part), 71), part),
        "key_up": gaussian(splits[3], (LAT, H, NOPE), LAT ** -0.5, 0.25, ((1, 16),)),
        "value_up": gaussian(splits[4], (LAT, H, VD), LAT ** -0.5, 0.25, ((1, 16),)),
        "first_key": draw_first_key(jax.random.fold_in(jax.random.fold_in(splits[7], part), 71), part),
        "out_grad": gaussian(own_keys[6], (SEQ, H, VD), 1.0, 6.0, ((0, 16),)),
    }


def reference(queries, latent, rope_key, key_up, value_up, first_key, out_grad):
    wide = jnp.float32
    low = jnp.bfloat16
    score_scale = 1.0 / math.sqrt(QK)
    latent_wide = latent.astype(wide)
    key_nope = jnp.einsum('tc,chd->thd', latent_wide, key_up.astype(wide)).astype(low)
    values = jnp.einsum('tc,chd->thd', latent_wide, value_up.astype(wide)).astype(low)
    keys_all = jnp.concatenate([key_nope, jnp.broadcast_to(rope_key[:, None, :], (SEQ, H, ROPE))], axis=2)
    window = QBLOCK + SPAN
    block_count = SEQ // QBLOCK

    def backward_block(carry, block_index):
        key_grad, value_grad = carry
        first_row = (block_index * QBLOCK).astype(jnp.int32)
        first_col = jnp.maximum(first_row - SPAN, 0).astype(jnp.int32)
        query_block = lax.dynamic_slice_in_dim(queries, first_row, QBLOCK, 0).astype(wide)
        grad_block = lax.dynamic_slice_in_dim(out_grad, first_row, QBLOCK, 0).astype(wide)
        key_block = lax.dynamic_slice_in_dim(keys_all, first_col, window, 0).astype(wide)
        value_block = lax.dynamic_slice_in_dim(values, first_col, window, 0).astype(wide)
        limits = lax.dynamic_slice_in_dim(first_key, first_row, QBLOCK, 0)
        row_pos = first_row + jnp.arange(QBLOCK, dtype=jnp.int32)
        col_pos = first_col + jnp.arange(window, dtype=jnp.int32)
        visible = (col_pos[None, :] >= limits[:, None]) & (col_pos[None, :] <= row_pos[:, None])
        scores = jnp.einsum('ihd,jhd->hij', query_block, key_block) * score_scale
        scores = jnp.where(visible[None], scores, -jnp.inf)
        peak = lax.optimization_barrier(jnp.max(scores, axis=2, keepdims=True))
        log_total = peak + jnp.log(lax.optimization_barrier(jnp.sum(jnp.exp(scores - peak), axis=2, keepdims=True)))
        probs = jnp.exp(scores - log_total)
        probs_low = probs.astype(low).astype(wide)
        attended = jnp.einsum('hij,jhd->ihd', probs_low, value_block)
        delta = lax.optimization_barrier(jnp.sum(grad_block * attended, axis=2)).T[:, :, None]
        prob_grad = jnp.einsum('ihd,jhd->hij', grad_block, value_block)
        score_grad = (probs * (prob_grad - delta)).astype(low).astype(wide)
        block_qgrad = (score_scale * jnp.einsum('hij,jhd->ihd', score_grad, key_block)).astype(low)
        block_kgrad = score_scale * jnp.einsum('hij,ihd->jhd', score_grad, query_block)
        block_vgrad = jnp.einsum('hij,ihd->jhd', probs_low, grad_block)
        key_grad = lax.dynamic_update_slice_in_dim(key_grad, lax.dynamic_slice_in_dim(key_grad, first_col, window, 0) + block_kgrad, first_col, 0)
        value_grad = lax.dynamic_update_slice_in_dim(value_grad, lax.dynamic_slice_in_dim(value_grad, first_col, window, 0) + block_vgrad, first_col, 0)
        return ((key_grad, value_grad), block_qgrad)
    start = (jnp.zeros((SEQ, H, QK), wide), jnp.zeros((SEQ, H, VD), wide))
    (key_grad, value_grad), query_blocks = lax.scan(backward_block, start, jnp.arange(block_count, dtype=jnp.int32))
    query_grad = query_blocks.reshape(SEQ, H, QK)
    key_low = key_grad.astype(low).astype(wide)
    value_low = value_grad.astype(low).astype(wide)
    key_part = key_low[:, :, :NOPE]
    key_up_grad = jnp.einsum('tc,thd->chd', latent_wide, key_part)
    value_up_grad = jnp.einsum('tc,thd->chd', latent_wide, value_low)
    latent_grad = jnp.einsum('thd,chd->tc', key_part, key_up.astype(wide)) + jnp.einsum('thd,chd->tc', value_low, value_up.astype(wide))
    rope_key_grad = lax.optimization_barrier(jnp.sum(key_low[:, :, NOPE:], axis=1))
    return (query_grad, latent_grad.astype(low), rope_key_grad.astype(low), key_up_grad, value_up_grad)
```

```python
import functools
import math

import jax
import jax.numpy as jnp
from jax import lax
from jax.experimental import pallas as pl
from jax.experimental.pallas import tpu as pltpu
from jax.sharding import PartitionSpec as P

WIDE = jnp.float32
LOW = jnp.bfloat16
MESH = pl.DeviceIdType.MESH
NT = (((1,), (1,)), ((), ()))


def dot(a, b):
    return jnp.dot(a, b, preferred_element_type=WIDE)


def dot_nt(a, b):
    return lax.dot_general(a, b, NT, preferred_element_type=WIDE)


def kernel(
    n, scale,
    x_ref, l_ref, w_ref, fk_ref,
    y_ref, g_ref, ku_ref, vu_ref,
    xr, la, lat, kk, kt, vv, kg, vg, lp, rp, ys, ls, lr,
    sx, rx, sl, rl, sy, ry, sg, rg, lsem, osem,
):
    me = lax.axis_index("head")
    pairs, rows, lanes = x_ref.shape[1], x_ref.shape[3], x_ref.shape[4]
    width = l_ref.shape[1] - lanes
    seq = n * rows
    block = 2 * rows
    reach = 4 * rows
    window = block + reach
    half = lanes // 2

    def peers(body):
        def step(k, _):
            body(lax.rem(me + k, n))
            return 0

        lax.fori_loop(1, n, step, 0)

    def remote(src, dst, send, recv, peer):
        return pltpu.make_async_remote_copy(
            src_ref=src, dst_ref=dst, send_sem=send, recv_sem=recv,
            device_id={"head": peer}, device_id_type=MESH,
        )

    def copy_l(src_dev, peer):
        return remote(l_ref, la.at[pl.ds(src_dev * rows, rows)],
                      sl.at[peer], rl.at[src_dev], peer)

    spans = (pl.ds(0, 3), pl.ds(3, 2))

    def copy_x(pair, odd, src_dev, peer):
        return remote(x_ref.at[peer, pair, spans[odd]], xr.at[src_dev, pair, spans[odd]],
                      sx.at[2 * pair + odd, peer], rx.at[2 * pair + odd, src_dev], peer)

    outs = (pl.ds(0, 1), pl.ds(1, 2))

    def copy_y(pair, odd, src_dev, peer):
        return remote(ys.at[peer, pair, outs[odd]], y_ref.at[src_dev, pair, outs[odd]],
                      sy.at[2 * pair + odd, peer], ry.at[2 * pair + odd, src_dev], peer)

    def copy_g(src_dev, peer):
        return remote(ls.at[pl.ds(peer * rows, rows)], lr.at[src_dev],
                      sg.at[peer], rg.at[src_dev], peer)

    own_l = pltpu.make_async_copy(l_ref, la.at[pl.ds(me * rows, rows)], lsem.at[0])
    own_x = pltpu.make_async_copy(x_ref.at[me], xr.at[me], lsem.at[1])
    own_l.start()
    own_x.start()

    barrier = pltpu.get_barrier_semaphore()
    peers(lambda p: pl.semaphore_signal(
        barrier, inc=1, device_id={"head": p}, device_id_type=MESH))
    pl.semaphore_wait(barrier, n - 1)

    peers(lambda p: copy_l(me, p).start())

    def send_pair(pair, _):
        for odd in range(2):
            peers(lambda p: copy_x(pair, odd, me, p).start())
        return 0

    lax.fori_loop(0, pairs, send_pair, 0)

    kk[pl.ds(0, reach), :] = jnp.zeros((reach, 2 * lanes), LOW)
    kt[:, pl.ds(0, reach)] = jnp.zeros((2 * lanes, reach), LOW)
    vv[pl.ds(0, reach), :] = jnp.zeros((reach, lanes), LOW)
    low_half = lax.broadcasted_iota(jnp.int32, (block, lanes), 1) < half

    own_l.wait()
    peers(lambda p: copy_l(p, p).wait_recv())
    own_x.wait()

    def flip(t, _):
        at = pl.ds(pl.multiple_of(t * block, block), block)
        lat[:, at] = la[at, pl.ds(0, width)].T
        rp[at, :] = jnp.zeros((block, lanes), WIDE)
        lp[at, :] = jnp.zeros((block, width), WIDE)
        return 0

    lax.fori_loop(0, seq // block, flip, 0)

    def clear(t, _):
        at = pl.ds(pl.multiple_of(t * block, block), block)
        kg[at, :] = jnp.zeros((block, 2 * lanes), WIDE)
        vg[at, :] = jnp.zeros((block, lanes), WIDE)
        return 0

    def one_head(pair, odd):
        head = 2 * pair + odd
        keep = jnp.logical_not(low_half) if odd else low_half
        zero_low = jnp.zeros((block, lanes), WIDE)

        def expand(t, _):
            at = pl.ds(pl.multiple_of(t * block, block), block)
            to = pl.ds(pl.multiple_of(t * block + reach, block), block)
            both = dot(la[at, pl.ds(0, width)], w_ref[head])
            rope = jnp.where(keep, la[at, pl.ds(width, lanes)].astype(WIDE), zero_low)
            keys = jnp.concatenate([both[:, :lanes], rope], axis=1)
            kk[to, :] = keys.astype(LOW)
            kt[:, to] = keys.T.astype(LOW)
            vv[to, :] = both[:, lanes:].astype(LOW)
            return 0

        lax.fori_loop(0, seq // block, expand, 0)
        lax.fori_loop(0, (seq + reach) // block, clear, 0)
        peers(lambda p: copy_x(pair, odd, p, p).wait_recv())

        def attend(b, _):
            start = pl.multiple_of(b * block, block)
            win = pl.ds(start, window)
            src = pl.ds(2 * b, 2)
            nope = xr[src, pair, 1 + 2 * odd].reshape(block, lanes)
            grad = xr[src, pair, 2 + 2 * odd].reshape(block, lanes)
            rope = xr[src, pair, 0].reshape(block, lanes)
            q = jnp.concatenate([nope, rope], axis=1)
            s = dot_nt(kk[win, :], q)
            pg = dot_nt(vv[win, :], grad)
            col = lax.broadcasted_iota(jnp.int32, (window, block), 0) + (start - reach)
            row = lax.broadcasted_iota(jnp.int32, (1, block), 1) + start
            first = fk_ref[:, pl.ds(start, block)]
            s = jnp.where((col >= first) & (col <= row), s, -jnp.inf)
            peak = jnp.max(s, axis=0, keepdims=True)
            e = jnp.exp2((s - peak) * (scale * math.log2(math.e)))
            inv = 1.0 / jnp.sum(e, axis=0, keepdims=True)
            delta = jnp.sum(e * pg, axis=0, keepdims=True) * inv
            p = e * inv
            ds = (p * (pg - delta)).astype(LOW)
            vg[win, :] += dot(p.astype(LOW), grad)
            kg[win, :] += dot(ds, q)
            qg = (dot(kt[:, win], ds) * scale).T.astype(LOW)
            ys[src, pair, odd] = qg[:, :lanes].reshape(2, rows, lanes)
            if odd:
                other = ys[src, pair, 2].reshape(block, lanes)
                rope_out = jnp.where(low_half, other.astype(WIDE), qg[:, lanes:].astype(WIDE))
                ys[src, pair, 2] = rope_out.astype(LOW).reshape(2, rows, lanes)
            else:
                ys[src, pair, 2] = qg[:, lanes:].reshape(2, rows, lanes)
            return 0

        lax.fori_loop(0, n // 2, attend, 0)
        peers(lambda p: copy_y(pair, odd, me, p).start())

        def finish(t, carry):
            ku, vu = carry
            at = pl.ds(pl.multiple_of(t * block, block), block)
            frm = pl.ds(pl.multiple_of(t * block + reach, block), block)
            keys = kg[frm, :] * scale
            low = jnp.concatenate([keys[:, :lanes].astype(LOW), vg[frm, :].astype(LOW)], axis=1)
            rope = keys[:, lanes:].astype(LOW).astype(WIDE)
            rp[at, :] += jnp.where(keep, rope, zero_low)
            lp[at, :] += dot_nt(low, w_ref[head])
            up = dot(lat[:, at], low)
            return ku + up[:, :lanes], vu + up[:, lanes:]

        zero = jnp.zeros((width, lanes), WIDE)
        ku, vu = lax.fori_loop(0, seq // block, finish, (zero, zero))
        ku_ref[head] = ku
        vu_ref[head] = vu

    def both_heads(pair, _):
        one_head(pair, 0)
        one_head(pair, 1)
        return 0

    lax.fori_loop(0, pairs, both_heads, 0)
    own_y = pltpu.make_async_copy(ys.at[me], y_ref.at[me], osem)
    own_y.start()

    def pack(t, _):
        at = pl.ds(pl.multiple_of(t * block, block), block)
        ls[at, pl.ds(0, width)] = lp[at, :].astype(LOW)
        ls[at, pl.ds(width, lanes)] = rp[at, :].astype(LOW)
        return 0

    lax.fori_loop(0, seq // block, pack, 0)
    peers(lambda p: copy_g(me, p).start())

    def add(k, total):
        p = lax.rem(me + k, n)
        copy_g(p, p).wait_recv()
        return total + lr[p].astype(WIDE)

    total = ls[pl.ds(me * rows, rows), :].astype(WIDE)
    g_ref[...] = lax.fori_loop(1, n, add, total)

    own_y.wait()
    peers(lambda p: copy_l(me, p).wait_send())
    peers(lambda p: copy_g(me, p).wait_send())

    def drain(pair, _):
        for odd in range(2):
            peers(lambda p: copy_x(pair, odd, me, p).wait_send())
            peers(lambda p: copy_y(pair, odd, me, p).wait_send())
            peers(lambda p: copy_y(pair, odd, p, p).wait_recv())
        return 0

    lax.fori_loop(0, pairs, drain, 0)


def shards(queries, latent, rope_key, key_up, value_up, first_key, out_grad):
    n = lax.axis_size("head")
    rows, all_heads, qk = queries.shape
    width, heads, nope = key_up.shape
    rope = qk - nope
    lanes = out_grad.shape[2]
    pairs = heads // 2
    seq = rows * n
    reach = 4 * rows
    scale = 1.0 / math.sqrt(qk)

    q = queries.reshape(rows, n, pairs, 2, qk)
    d = out_grad.reshape(rows, n, pairs, 2, lanes)
    q_rope = q[..., nope:].reshape(rows, n, pairs, 2 * rope)
    x = jnp.stack(
        [q_rope, q[:, :, :, 0, :nope], d[:, :, :, 0], q[:, :, :, 1, :nope], d[:, :, :, 1]],
        axis=3,
    ).transpose(1, 2, 3, 0, 4)
    lcat = jnp.concatenate([latent, rope_key, rope_key], axis=1)
    w = jnp.concatenate([key_up, value_up], axis=2).transpose(1, 0, 2)

    any_spec = pl.BlockSpec(memory_space=pl.ANY)
    vmem = pl.BlockSpec(memory_space=pltpu.VMEM)
    dma = pltpu.SemaphoreType.DMA
    total_w = width + lanes
    y, g, ku, vu = pl.pallas_call(
        functools.partial(kernel, n, scale),
        out_shape=[
            jax.ShapeDtypeStruct((n, pairs, 3, rows, lanes), LOW),
            jax.ShapeDtypeStruct((rows, total_w), WIDE),
            jax.ShapeDtypeStruct((heads, width, lanes), WIDE),
            jax.ShapeDtypeStruct((heads, width, lanes), WIDE),
        ],
        in_specs=[any_spec, any_spec, vmem, vmem],
        out_specs=[any_spec, vmem, vmem, vmem],
        scratch_shapes=[
            pltpu.VMEM((n, pairs, 5, rows, lanes), LOW),
            pltpu.VMEM((seq, total_w), LOW),
            pltpu.VMEM((width, seq), LOW),
            pltpu.VMEM((reach + seq, 2 * lanes), LOW),
            pltpu.VMEM((2 * lanes, reach + seq), LOW),
            pltpu.VMEM((reach + seq, lanes), LOW),
            pltpu.VMEM((reach + seq, 2 * lanes), WIDE),
            pltpu.VMEM((reach + seq, lanes), WIDE),
            pltpu.VMEM((seq, width), WIDE),
            pltpu.VMEM((seq, lanes), WIDE),
            pltpu.VMEM((n, pairs, 3, rows, lanes), LOW),
            pltpu.VMEM((seq, total_w), LOW),
            pltpu.VMEM((n, rows, total_w), LOW),
            dma((heads, n)), dma((heads, n)),
            dma((n,)), dma((n,)),
            dma((heads, n)), dma((heads, n)),
            dma((n,)), dma((n,)),
            dma((2,)), dma,
        ],
        compiler_params=pltpu.CompilerParams(
            collective_id=0, has_side_effects=True, vmem_limit_bytes=62 * 1024 * 1024
        ),
    )(x, lcat, w, first_key.reshape(1, seq))

    y_nope = y[:, :, :2].transpose(3, 0, 1, 2, 4)
    y_rope = y[:, :, 2].transpose(2, 0, 1, 3).reshape(rows, n, pairs, 2, rope)
    query_out = jnp.concatenate([y_nope, y_rope], axis=4).reshape(rows, all_heads, qk)
    latent_grad = g[:, :width].astype(LOW)
    rope_grad = (g[:, width : width + rope] + g[:, width + rope :]).astype(LOW)
    return (query_out, latent_grad, rope_grad, ku.transpose(1, 0, 2), vu.transpose(1, 0, 2))


def solution(mesh):
    return jax.shard_map(
        shards,
        mesh=mesh,
        in_specs=(
            P(("group", "head"), None, None),
            P(("group", "head"), None),
            P(("group", "head"), None),
            P(None, "head", None),
            P(None, "head", None),
            P("group"),
            P(("group", "head"), None, None),
        ),
        out_specs=(
            P(("group", "head"), None, None),
            P(("group", "head"), None),
            P(("group", "head"), None),
            P("group", "head", None),
            P("group", "head", None),
        ),
        check_vma=False,
    )
```
